128 devices in a mesh: inner: 8 (over x_lo, y), outer: 8 (over z, core), head: 2 (over x_hi).
Axes of the slice: x: 4 (x_hi: 2, x_lo: 2; x = x_hi * 2 + x_lo), y: 4, z: 4, core: 2. Of those that a mesh axis runs over, the one named last changes fastest.
Arguments:
- queries: bfloat16 [16384, 3072], P(('inner', 'outer', 'head')), may hold values from -5 to 5
- keys: bfloat16 [16384, 512], P(('inner', 'outer', 'head')), may hold values from -5 to 5
- values: bfloat16 [16384, 512], P(('inner', 'outer', 'head')), may hold values from -6 to 6
- output_gradient: bfloat16 [16384, 3072], P(('inner', 'outer', 'head')), may hold values from -6 to 6
- span_order: int32 [128], replicated, may hold values from 0 to 127, each once
Outputs:
- grad_q: bfloat16 [16384, 3072], P(('inner', 'outer', 'head'))
- key_gradient_out: bfloat16 [16384, 512], P(('inner', 'outer', 'head'))
- value_gradient_out: bfloat16 [16384, 512], P(('inner', 'outer', 'head'))
The draws below stay inside these ranges and needn't reach their ends.
Inputs may be any that keep to these rules, and one draw needn't show every extreme that they name: A permutation; storage rows j * 128 to (j + 1) * 128 - 1 hold the sequence positions span_order[j] * 128 onward.
All inputs are finite; a program needn't handle non-finite values.
Results may differ from the reference program's by a relative error of at most 0.0077.
Values may be sent and summed in bfloat16 or wider, within the bound.
No kernel may reach another device: no remote copies, remote signals or barrier semaphores. Data moves between devices by JAX's collectives and lax.ppermute only.
A program may use at most 192 MiB of HBM per device.

```python
import math
import jax
import jax.numpy as jnp
from jax import lax

QUERY_HEADS = 24
KEY_VALUE_HEADS = 4
HEAD_SIZE = 128
INNER_WIN = 4
OUTER_WIN = 2
TOKENS_PER_PAIR = 256
SPAN = 128
SEQUENCE_TOKENS = 16384
NCHUNK = 128
N_INNER = 8
N_OUTER = 8


def draw_queries(key, part):
    key = jax.random.fold_in(key, 1)
    heads_per_group = QUERY_HEADS // KEY_VALUE_HEADS
    start_offset = jnp.clip(jax.random.normal(key, (SEQUENCE_TOKENS, KEY_VALUE_HEADS, heads_per_group, HEAD_SIZE), jnp.float32), -5.0, 5.0)
    return start_offset.reshape(SEQUENCE_TOKENS, QUERY_HEADS * HEAD_SIZE).astype(jnp.bfloat16)


def draw_keys(key, part):
    key = jax.random.fold_in(key, 2)
    start_offset = jnp.clip(jax.random.normal(key, (SEQUENCE_TOKENS, KEY_VALUE_HEADS, HEAD_SIZE), jnp.float32), -5.0, 5.0)
    return start_offset.reshape(SEQUENCE_TOKENS, KEY_VALUE_HEADS * HEAD_SIZE).astype(jnp.bfloat16)


def level_of(rng, dims, shards, low, high):
    level = 1.0
    for dim, shards_of in shards:
        steps = jax.random.uniform(jax.random.fold_in(jax.random.fold_in(rng, 6), dim), (shards_of,), jnp.float32, low / len(shards), high / len(shards))
        level = level * jnp.repeat(jnp.exp(steps), dims[dim] // shards_of).reshape((-1,) + (1,) * (len(dims) - 1 - dim))
    return level


def normal_values(stream_key, shape, scale, reach, split=(), kind=jnp.bfloat16):
    gain = level_of(stream_key, shape, split, -0.22, 0.18) if split else 1.0
    entries = jax.random.normal(stream_key, shape, jnp.float32) * scale * gain
    return jnp.minimum(jnp.maximum(entries, -reach), reach).astype(kind)


def setup_inputs(seed: int = 0) -> dict:
    key_of = jax.random.split(jax.random.key(seed), 6)
    queries = draw_queries(jax.random.fold_in(key_of[5], 71), 0)
    keys = draw_keys(jax.random.fold_in(key_of[5], 71), 0)
    values = normal_values(key_of[2], (SEQUENCE_TOKENS, KEY_VALUE_HEADS * HEAD_SIZE), 1.0, 6.0, ((0, 128),))
    output_gradient = normal_values(key_of[3], (SEQUENCE_TOKENS, QUERY_HEADS * HEAD_SIZE), 1.0, 6.0, ((0, 128),))
    span_order = jax.random.permutation(key_of[4], NCHUNK).astype(jnp.int32)
    return dict(queries=queries, keys=keys, values=values, output_gradient=output_gradient, span_order=span_order)


def reference(queries, keys, values, output_gradient, span_order):
    heads_per_group = QUERY_HEADS // KEY_VALUE_HEADS
    score_scaling_factor = 1.0 / math.sqrt(HEAD_SIZE)
    count_of_blocks = N_INNER * N_OUTER
    window_width = INNER_WIN * OUTER_WIN
    row_index = jnp.arange(SEQUENCE_TOKENS, dtype=jnp.int32)
    position = span_order[row_index // SPAN] * SPAN + row_index % SPAN
    key_block_list = keys.astype(jnp.float32).reshape(count_of_blocks, TOKENS_PER_PAIR, KEY_VALUE_HEADS, HEAD_SIZE)
    value_block_list = values.astype(jnp.float32).reshape(count_of_blocks, TOKENS_PER_PAIR, KEY_VALUE_HEADS, HEAD_SIZE)
    query_block_list = queries.astype(jnp.float32).reshape(count_of_blocks, TOKENS_PER_PAIR, KEY_VALUE_HEADS, heads_per_group, HEAD_SIZE)
    gradient_block_list = output_gradient.astype(jnp.float32).reshape(count_of_blocks, TOKENS_PER_PAIR, KEY_VALUE_HEADS, heads_per_group, HEAD_SIZE)
    pos_blocks = position.reshape(count_of_blocks, TOKENS_PER_PAIR)
    inner_off = jnp.repeat(jnp.arange(INNER_WIN, dtype=jnp.int32), OUTER_WIN)
    outer_off = jnp.tile(jnp.arange(OUTER_WIN, dtype=jnp.int32), INNER_WIN)

    def one_block(carried, block_data):
        query_head_rows, gradient_head_list, query_pos, block_id = block_data
        block_inner = block_id // N_OUTER
        block_outer = block_id % N_OUTER
        source_blocks = ((block_inner - inner_off) % N_INNER * N_OUTER + (block_outer - outer_off) % N_OUTER).astype(jnp.int32)
        every_key = key_block_list[source_blocks].reshape(window_width * TOKENS_PER_PAIR, KEY_VALUE_HEADS, HEAD_SIZE)
        every_value = value_block_list[source_blocks].reshape(window_width * TOKENS_PER_PAIR, KEY_VALUE_HEADS, HEAD_SIZE)
        key_pos = pos_blocks[source_blocks].reshape(window_width * TOKENS_PER_PAIR)
        scores = jnp.einsum('qhgd,khd->hgqk', query_head_rows, every_key) * score_scaling_factor
        visible = key_pos[None, :] <= query_pos[:, None]
        scores = jnp.where(visible[None, None], scores, -jnp.inf)
        row_max = lax.optimization_barrier(jnp.max(scores, axis=-1))
        row_total = lax.optimization_barrier(jnp.sum(jnp.exp(scores - row_max[..., None]), axis=-1))
        log_total = row_max + jnp.log(row_total)
        weights = jnp.exp(scores - log_total[..., None])
        grad_dot = jnp.einsum('qhgd,khd->hgqk', gradient_head_list, every_value)
        row_dot = lax.optimization_barrier(jnp.sum(weights * grad_dot, axis=-1))
        score_gradient = lax.optimization_barrier((weights * (grad_dot - row_dot[..., None])).astype(jnp.bfloat16)).astype(jnp.float32)
        weight_lower_precision = lax.optimization_barrier(weights.astype(jnp.bfloat16)).astype(jnp.float32)
        grad_query = (score_scaling_factor * jnp.einsum('hgqk,khd->qhgd', score_gradient, every_key)).astype(jnp.bfloat16)
        key_gradient_sum, value_gradient_sum = carried
        key_gradient_term = jnp.einsum('emts,temc->sec', score_gradient, query_head_rows).reshape(window_width, TOKENS_PER_PAIR, KEY_VALUE_HEADS, HEAD_SIZE)
        value_gradient_term = jnp.einsum('emts,temc->sec', weight_lower_precision, gradient_head_list).reshape(window_width, TOKENS_PER_PAIR, KEY_VALUE_HEADS, HEAD_SIZE)
        key_gradient_sum = key_gradient_sum.at[source_blocks].add(key_gradient_term)
        value_gradient_sum = value_gradient_sum.at[source_blocks].add(value_gradient_term)
        return ((key_gradient_sum, value_gradient_sum), grad_query)
    zero_initial = jnp.zeros((count_of_blocks, TOKENS_PER_PAIR, KEY_VALUE_HEADS, HEAD_SIZE), jnp.float32)
    block_ids = jnp.arange(count_of_blocks, dtype=jnp.int32)
    (key_gradient_sum, value_gradient_sum), grad_query = lax.scan(one_block, (zero_initial, zero_initial), (query_block_list, gradient_block_list, pos_blocks, block_ids))
    grad_q = grad_query.reshape(SEQUENCE_TOKENS, QUERY_HEADS * HEAD_SIZE)
    key_gradient_out = (score_scaling_factor * key_gradient_sum).astype(jnp.bfloat16).reshape(SEQUENCE_TOKENS, KEY_VALUE_HEADS * HEAD_SIZE)
    value_gradient_out = value_gradient_sum.astype(jnp.bfloat16).reshape(SEQUENCE_TOKENS, KEY_VALUE_HEADS * HEAD_SIZE)
    return (grad_q, key_gradient_out, value_gradient_out)
```

```python
import functools
import math

import jax
import jax.numpy as jnp
from jax import lax
from jax.experimental import pallas as pl
from jax.experimental.pallas import tpu as pltpu
from jax.sharding import PartitionSpec as P

HEAD = 128
GROUP = 6
KV = 2
WIN = 4
SPAN = 128
COLS = 2 * GROUP * HEAD
Y = 4
NEG = -1e30
SCALE = 1.0 / math.sqrt(HEAD)
SCALE2 = SCALE * math.log2(math.e)
NT = (((1,), (1,)), ((), ()))
NN = (((1,), (0,)), ((), ()))


def dot(a, b, dims):
    return lax.dot_general(a, b, dims, preferred_element_type=jnp.float32)


def attention_kernel(order, q_own, q_far, do_own, do_far, *refs):
    kv = refs[:8]
    dq_own, dq_far = refs[8:10]
    dkv = refs[10:18]
    s_scr, dp_scr, p_scr, ds_scr, kt_scr, q_scr, do_scr = refs[18:]
    inner, outer, head = lax.axis_index("inner"), lax.axis_index("outer"), lax.axis_index("head")

    def span_of(d, o, half):
        block = lax.rem(inner + 8 - d, 8) * 8 + lax.rem(outer + 8 - o, 8)
        return order[block * 2 + (head if half == 0 else 1 - head)]

    lane = lax.broadcasted_iota(jnp.int32, (1, 256), 1)
    at = [span_of(0, 0, 0), span_of(0, 0, 1)]
    hidden = []
    for n in range(8):
        for half in range(2):
            key = span_of(n % WIN, n // WIN, half)
            first = jnp.where(key <= at[0], 0.0, -NEG)
            second = jnp.where(key <= at[1], 0.0, -NEG)
            hidden.append(jnp.where(lane < SPAN, first, second).astype(jnp.float32))
    row = lax.broadcasted_iota(jnp.int32, (256, 256), 0)
    col = lax.broadcasted_iota(jnp.int32, (256, 256), 1)
    key_pos = jnp.where(row < SPAN, at[0], at[1]) * SPAN + (row & (SPAN - 1))
    row_pos = jnp.where(col < SPAN, at[0], at[1]) * SPAN + (col & (SPAN - 1))
    own_visible = key_pos <= row_pos

    for j in range(KV):
        k_at = slice(j * HEAD, (j + 1) * HEAD)
        v_at = slice((KV + j) * HEAD, (KV + j + 1) * HEAD)
        for n in range(8):
            kt_scr[:, n * 256 : (n + 1) * 256] = kv[n][:, k_at].T

        def one_head(g, carry):
            at_h = pl.ds(pl.multiple_of((j * GROUP + g) * HEAD, HEAD), HEAD)
            rows = pl.ds(pl.multiple_of(g * 256, 256), 256)
            q_h = jnp.concatenate([q_own[:, at_h], q_far[:, at_h]], axis=0)
            do_h = jnp.concatenate([do_own[:, at_h], do_far[:, at_h]], axis=0)
            q_scr[rows, :] = q_h
            do_scr[rows, :] = do_h
            top = jnp.full((1, 256), NEG, jnp.float32)
            for n in range(8):
                s = dot(kv[n][:, k_at], q_h, NT)
                if n == 0:
                    s = jnp.where(own_visible, s, NEG)
                s_scr[n * 256 : (n + 1) * 256, :] = s
                for half in range(2):
                    here = jnp.max(s[half * 128 : (half + 1) * 128], axis=0, keepdims=True)
                    top = jnp.maximum(top, here - hidden[2 * n + half] if n else here)
            top = top * SCALE2
            total = jnp.zeros((8, 256), jnp.float32)
            row_dot = jnp.zeros((8, 256), jnp.float32)
            for n in range(8):
                dp = dot(kv[n][:, v_at], do_h, NT)
                dp_scr[n * 256 : (n + 1) * 256, :] = dp
                for half in range(2):
                    at_r = slice(n * 256 + half * 128, n * 256 + half * 128 + 128)
                    lower = top + hidden[2 * n + half] if n else top
                    e = jnp.exp2(s_scr[at_r, :] * SCALE2 - lower)
                    s_scr[at_r, :] = e
                    total = total + jnp.sum(e.reshape(16, 8, 256), axis=0)
                    product = e * dp[half * 128 : (half + 1) * 128]
                    row_dot = row_dot + jnp.sum(product.reshape(16, 8, 256), axis=0)
            inverse = 1.0 / jnp.sum(total, axis=0, keepdims=True)
            row_dot = jnp.sum(row_dot, axis=0, keepdims=True) * inverse
            dq_t = jnp.zeros((HEAD, 256), jnp.float32)
            for n in range(8):
                at_r = slice(n * 256, (n + 1) * 256)
                p = s_scr[at_r, :] * inverse
                ds = (p * (dp_scr[at_r, :] - row_dot)).astype(jnp.bfloat16)
                p_scr[at_r, rows] = p.astype(jnp.bfloat16)
                ds_scr[at_r, rows] = ds
                dq_t = dq_t + dot(kt_scr[:, at_r], ds, NN)
            dq = (dq_t * SCALE).T.astype(jnp.bfloat16)
            dq_own[:, at_h] = dq[:SPAN]
            dq_far[:, at_h] = dq[SPAN:]
            return carry

        lax.fori_loop(0, GROUP, one_head, 0)
        for n in range(8):
            at_r = slice(n * 256, (n + 1) * 256)
            dk = dot(ds_scr[at_r, :], q_scr[...], NN) * SCALE
            dv = dot(p_scr[at_r, :], do_scr[...], NN)
            dkv[n][:, k_at] = dk.astype(jnp.bfloat16)
            dkv[n][:, v_at] = dv.astype(jnp.bfloat16)


def attention(order, q_own, q_far, do_own, do_far, blocks):
    vmem = pl.BlockSpec(memory_space=pltpu.VMEM)
    rows = jax.ShapeDtypeStruct((SPAN, COLS), jnp.bfloat16)
    block = jax.ShapeDtypeStruct((256, 512), jnp.bfloat16)
    out = pl.pallas_call(
        attention_kernel,
        in_specs=[pl.BlockSpec(memory_space=pltpu.SMEM)] + [vmem] * 12,
        out_specs=[vmem] * 10,
        out_shape=[rows] * 2 + [block] * 8,
        scratch_shapes=[
            pltpu.VMEM((2048, 256), jnp.float32),
            pltpu.VMEM((2048, 256), jnp.float32),
            pltpu.VMEM((2048, GROUP * 256), jnp.bfloat16),
            pltpu.VMEM((2048, GROUP * 256), jnp.bfloat16),
            pltpu.VMEM((HEAD, 2048), jnp.bfloat16),
            pltpu.VMEM((GROUP * 256, HEAD), jnp.bfloat16),
            pltpu.VMEM((GROUP * 256, HEAD), jnp.bfloat16),
        ],
        compiler_params=pltpu.CompilerParams(vmem_limit_bytes=48 * 1024 * 1024),
        cost_estimate=pl.CostEstimate(
            flops=10 * 12 * 256 * 2048 * 128, bytes_accessed=10_000_000, transcendentals=12 * 256 * 2048
        ),
    )(order, q_own, q_far, do_own, do_far, *blocks)
    return out[0], out[1], out[2:]


def to_partner(x):
    return lax.ppermute(x, "head", [(0, 1), (1, 0)])


def to_column(x, flip, rows=(0, 1, 2, 3)):
    perm = []
    for lo in range(2):
        for y in rows:
            for h in range(2):
                perm.append(((lo * Y + y) * 2 + h, ((1 - lo) * Y + y) * 2 + (h ^ flip)))
    return lax.ppermute(x, ("inner", "head"), perm)


def along_y(x, by):
    return lax.ppermute(
        x, "inner", [(lo * Y + y, lo * Y + (y + by) % Y) for lo in range(2) for y in range(Y)]
    )


def along_outer(x, by):
    return lax.ppermute(x, "outer", [(o, (o + by) % 8) for o in range(8)])


def f32(x):
    return x.astype(jnp.float32)


def shards(queries, keys, values, output_gradient, span_order):
    head = lax.axis_index("head")
    y = lax.rem(lax.axis_index("inner"), Y)

    def cols(x, of, width):
        return lax.dynamic_slice_in_dim(x, of * width, width, axis=1)

    def piece(of):
        return jnp.concatenate([cols(keys, of, 256), cols(values, of, 256)], axis=1)

    mine, theirs = piece(head), piece(1 - head)
    own = jnp.concatenate([mine, to_partner(theirs)], axis=0)
    other = jnp.concatenate([to_column(mine, 0, (1, 2, 3)), to_column(theirs, 1, (1, 2, 3))], axis=0)
    q_own, do_own = cols(queries, head, COLS), cols(output_gradient, head, COLS)
    q_far = to_partner(cols(queries, 1 - head, COLS))
    do_far = to_partner(cols(output_gradient, 1 - head, COLS))

    blocks = [own] + [along_y(jnp.where(y + k >= Y, other, own), k) for k in (1, 2, 3)]
    blocks = blocks + [along_outer(b, 1) for b in blocks]
    dq_own, dq_far, terms = attention(span_order, q_own, q_far, do_own, do_far, blocks)

    dq_back = to_partner(dq_far)
    sums = [
        (f32(terms[k]) + f32(along_outer(terms[WIN + k], -1))).astype(jnp.bfloat16)
        for k in range(WIN)
    ]
    own_sum = f32(sums[0])
    other_sum = jnp.zeros_like(own_sum)
    for k in (1, 2, 3):
        arrived = f32(along_y(sums[k], -k))
        own_sum = own_sum + jnp.where(y + k < Y, arrived, 0.0)
        other_sum = other_sum + jnp.where(y + k < Y, 0.0, arrived)
    other_sum = other_sum.astype(jnp.bfloat16)
    mine_sum = own_sum[:SPAN] + f32(to_column(other_sum[:SPAN], 0, (1, 2, 3)))
    theirs_sum = f32(to_partner(own_sum[SPAN:].astype(jnp.bfloat16))) + f32(
        to_column(other_sum[SPAN:], 1, (1, 2, 3))
    )
    mine_sum, theirs_sum = mine_sum.astype(jnp.bfloat16), theirs_sum.astype(jnp.bfloat16)

    def join(a, b):
        return jnp.where(
            head == 0, jnp.concatenate([a, b], axis=1), jnp.concatenate([b, a], axis=1)
        )

    return (
        join(dq_own, dq_back),
        join(mine_sum[:, :256], theirs_sum[:, :256]),
        join(mine_sum[:, 256:], theirs_sum[:, 256:]),
    )


def solution(mesh):
    rows = P(("inner", "outer", "head"), None)
    return jax.shard_map(
        shards,
        mesh=mesh,
        in_specs=(rows, rows, rows, rows, P()),
        out_specs=(rows, rows, rows),
        check_vma=False,
    )
```

```python
import functools
import math

import jax
import jax.numpy as jnp
from jax import lax
from jax.experimental import pallas as pl
from jax.experimental.pallas import tpu as pltpu
from jax.sharding import PartitionSpec as P

HEAD = 128
GROUP = 6
KV = 2
WIN = 4
SPAN = 128
COLS = GROUP * HEAD
Y = 4
NEG = -1e30
SCALE = 1.0 / math.sqrt(HEAD)
SCALE2 = SCALE * math.log2(math.e)
NT = (((1,), (1,)), ((), ()))
NN = (((1,), (0,)), ((), ()))
SMALL = pltpu.CompilerParams(vmem_limit_bytes=6 * 1024 * 1024)


def dot(a, b, dims):
    return lax.dot_general(a, b, dims, preferred_element_type=jnp.float32)


def attention_kernel(j, order, place, q_any, do_any, qf_any, dof_any, *refs):
    near_in, far_in = refs[:8], refs[8]
    dq_own, dq_far, near_out, far_out = refs[9:13]
    e_slots, dp_slots, p_scr, ds_scr, k_scr, v_scr, kt_scr, q_scr, do_scr = refs[13:22]
    block_scr, q_own, do_own, far, sems = refs[22:]
    inner, outer, head = place[0], place[1], place[2]
    my_cols = pl.ds(pl.multiple_of((head * KV + j) * COLS, COLS), COLS)
    copies = [
        pltpu.make_async_copy(near_in[n].at[j], block_scr.at[n], sems.at[n]) for n in range(8)
    ] + [
        pltpu.make_async_copy(far_in, block_scr.at[pl.ds(8, 8)], sems.at[8]),
        pltpu.make_async_copy(qf_any, far.at[pl.ds(0, SPAN)], sems.at[9]),
        pltpu.make_async_copy(dof_any, far.at[pl.ds(SPAN, SPAN)], sems.at[12]),
        pltpu.make_async_copy(q_any.at[:, my_cols], q_own, sems.at[10]),
        pltpu.make_async_copy(do_any.at[:, my_cols], do_own, sems.at[11]),
    ]
    for copy in copies:
        copy.start()

    def span_of(d, o, half):
        block = lax.rem(inner + 8 - d, 8) * 8 + lax.rem(outer + 8 - o, 8)
        return order[block * 2 + (head if half == 0 else 1 - head)]

    lane = lax.broadcasted_iota(jnp.int32, (1, 256), 1)
    at = [span_of(0, 0, 0), span_of(0, 0, 1)]
    hidden = []
    for n in range(8):
        for half in range(2):
            key = span_of(n % WIN, n // WIN, half)
            first = jnp.where(key <= at[0], 0.0, -NEG)
            second = jnp.where(key <= at[1], 0.0, -NEG)
            hidden.append(jnp.where(lane < SPAN, first, second).astype(jnp.float32))
    row = lax.broadcasted_iota(jnp.int32, (256, 256), 0)
    col = lax.broadcasted_iota(jnp.int32, (256, 256), 1)
    key_pos = jnp.where(row < SPAN, at[0], at[1]) * SPAN + (row & (SPAN - 1))
    row_pos = jnp.where(col < SPAN, at[0], at[1]) * SPAN + (col & (SPAN - 1))
    own_visible = key_pos <= row_pos

    for n in range(16):
        if n <= 8:
            copies[n].wait()
        both = block_scr[n]
        at_r = slice(n * SPAN, (n + 1) * SPAN)
        k_scr[at_r, :] = both[:, :HEAD]
        v_scr[at_r, :] = both[:, HEAD:]
        kt_scr[:, at_r] = both[:, :HEAD].T

    for copy in copies[9:]:
        copy.wait()
    for g in range(GROUP):
        at_h = slice(g * HEAD, (g + 1) * HEAD)
        rows = slice(g * 256, (g + 1) * 256)
        e_scr, dp_scr = e_slots.at[g % 2], dp_slots.at[g % 2]
        q_h = jnp.concatenate([q_own[:, at_h], far[:SPAN, at_h]], axis=0)
        do_h = jnp.concatenate([do_own[:, at_h], far[SPAN:, at_h]], axis=0)
        q_scr[rows, :] = q_h
        do_scr[rows, :] = do_h
        top = jnp.full((1, 256), NEG, jnp.float32)
        tops = []
        total = jnp.zeros((8, 256), jnp.float32)
        row_dot = jnp.zeros((8, 256), jnp.float32)
        for n in range(8):
            at_r = slice(n * 256, (n + 1) * 256)
            s = dot(k_scr[at_r, :], q_h, NT)
            if n == 0:
                s = jnp.where(own_visible, s, NEG)
            dp = dot(v_scr[at_r, :], do_h, NT)
            dp_scr[at_r, :] = dp
            before = top
            for half in range(2):
                here = jnp.max(s[half * 128 : (half + 1) * 128], axis=0, keepdims=True)
                top = jnp.maximum(top, (here - hidden[2 * n + half] if n else here) * SCALE2)
            tops.append(top)
            if n:
                decay = jnp.exp2(before - top)
                total, row_dot = total * decay, row_dot * decay
            for half in range(2):
                at_e = slice(n * 256 + half * 128, n * 256 + half * 128 + 128)
                lower = top + hidden[2 * n + half] if n else top
                e = jnp.exp2(s[half * 128 : (half + 1) * 128] * SCALE2 - lower)
                e_scr[at_e, :] = e
                total = total + jnp.sum(e.reshape(16, 8, 256), axis=0)
                product = e * dp[half * 128 : (half + 1) * 128]
                row_dot = row_dot + jnp.sum(product.reshape(16, 8, 256), axis=0)
        inverse = 1.0 / jnp.sum(total, axis=0, keepdims=True)
        row_dot = jnp.sum(row_dot, axis=0, keepdims=True) * inverse
        for n in range(8):
            at_r = slice(n * 256, (n + 1) * 256)
            p = e_scr[at_r, :] * (inverse * jnp.exp2(tops[n] - top))
            ds = p * (dp_scr[at_r, :] - row_dot)
            p_scr[at_r, rows] = p.astype(jnp.bfloat16)
            ds_scr[at_r, rows] = ds.astype(jnp.bfloat16)
    for n in range(8):
        at_r = slice(n * 256, (n + 1) * 256)
        dk = dot(ds_scr[at_r, :], q_scr[...], NN) * SCALE
        dv = dot(p_scr[at_r, :], do_scr[...], NN)
        out, at_o = (near_out if n < WIN else far_out), slice(n % WIN * 256, n % WIN * 256 + 256)
        out[at_o, :HEAD] = dk.astype(jnp.bfloat16)
        out[at_o, HEAD:] = dv.astype(jnp.bfloat16)
    for g in range(GROUP):
        dq = dot(kt_scr[...], ds_scr[:, g * 256 : (g + 1) * 256], NN) * SCALE
        dq = dq.T.astype(jnp.bfloat16)
        dq_own[:, g * HEAD : (g + 1) * HEAD] = dq[:SPAN]
        dq_far[:, g * HEAD : (g + 1) * HEAD] = dq[SPAN:]


def attention(j, order, place, queries, output_gradient, far, near_in, far_in):
    def whole(*shape):
        return pl.BlockSpec(shape, lambda i, order, place: (0,) * len(shape))

    hbm = pl.BlockSpec(memory_space=pltpu.HBM)
    free = pl.BlockSpec(memory_space=pl.ANY)
    rows = jax.ShapeDtypeStruct((SPAN, COLS), jnp.bfloat16)
    terms = jax.ShapeDtypeStruct((WIN * 256, 256), jnp.bfloat16)
    out = (rows, rows, terms, terms)
    return pl.pallas_call(
        functools.partial(attention_kernel, j),
        grid_spec=pltpu.PrefetchScalarGridSpec(
            num_scalar_prefetch=2,
            grid=(1,),
            in_specs=[hbm] * 4 + [free] * 8 + [hbm],
            out_specs=[whole(*o.shape) for o in out],
            scratch_shapes=[
                pltpu.VMEM((2, 2048, 256), jnp.float32),
                pltpu.VMEM((2, 2048, 256), jnp.float32),
                pltpu.VMEM((2048, GROUP * 256), jnp.bfloat16),
                pltpu.VMEM((2048, GROUP * 256), jnp.bfloat16),
                pltpu.VMEM((2048, HEAD), jnp.bfloat16),
                pltpu.VMEM((2048, HEAD), jnp.bfloat16),
                pltpu.VMEM((HEAD, 2048), jnp.bfloat16),
                pltpu.VMEM((GROUP * 256, HEAD), jnp.bfloat16),
                pltpu.VMEM((GROUP * 256, HEAD), jnp.bfloat16),
                pltpu.VMEM((16, SPAN, 256), jnp.bfloat16),
                pltpu.VMEM((SPAN, COLS), jnp.bfloat16),
                pltpu.VMEM((SPAN, COLS), jnp.bfloat16),
                pltpu.VMEM((256, COLS), jnp.bfloat16),
                pltpu.SemaphoreType.DMA((13,)),
            ],
        ),
        out_shape=out,
        compiler_params=pltpu.CompilerParams(vmem_limit_bytes=32 * 1024 * 1024),
        cost_estimate=pl.CostEstimate(
            flops=10 * 6 * 256 * 2048 * 128, bytes_accessed=5_000_000, transcendentals=6 * 256 * 2048
        ),
    )(order, place, queries, output_gradient, *far, *near_in, far_in)


def pack_kernel(*refs):
    halves, out = refs[:8], refs[9:11]
    for j in range(KV):
        for n in range(8):
            out[j][n] = halves[n][j]


def pack(near, after):
    vmem = pl.BlockSpec(memory_space=pltpu.VMEM)
    one = jax.ShapeDtypeStruct((8, SPAN, 256), jnp.bfloat16)
    return pl.pallas_call(
        pack_kernel,
        in_specs=[vmem] * 8 + [pl.BlockSpec(memory_space=pl.ANY)],
        out_specs=[vmem] * 2,
        out_shape=[one] * 2,
        compiler_params=SMALL,
    )(*near, after)


def tie_kernel(*refs):
    del refs


def tie(x, *after):
    free = pl.BlockSpec(memory_space=pl.ANY)
    return pl.pallas_call(
        tie_kernel,
        in_specs=[free] * (1 + len(after)),
        out_specs=free,
        out_shape=jax.ShapeDtypeStruct(x.shape, x.dtype),
        input_output_aliases={0: 0},
        compiler_params=SMALL,
    )(x, *after)


def join_rows_kernel(place, own0, own1, back0, back1, out):
    head = place[2]
    for x, h, j in ((own0, head, 0), (own1, head, 1), (back0, 1 - head, 0), (back1, 1 - head, 1)):
        out[:, pl.ds(pl.multiple_of((h * KV + j) * COLS, COLS), COLS)] = x[...]


def join_rows(place, own, back):
    vmem = pl.BlockSpec(memory_space=pltpu.VMEM)
    return pl.pallas_call(
        join_rows_kernel,
        in_specs=[pl.BlockSpec(memory_space=pltpu.SMEM)] + [vmem] * 4,
        out_specs=vmem,
        out_shape=jax.ShapeDtypeStruct((SPAN, 2 * KV * COLS), jnp.bfloat16),
        compiler_params=SMALL,
    )(place, *own, *back)


def cut_kernel(place, queries, output_gradient, after, *outs):
    del after
    for n, out in enumerate(outs):
        at = ((1 - place[2]) * KV + n // 2) * COLS
        at = pl.ds(pl.multiple_of(at, COLS), COLS)
        out[...] = (queries, output_gradient)[n % 2][:, at]


def cut(place, queries, output_gradient, after):
    vmem = pl.BlockSpec(memory_space=pltpu.VMEM)
    out = pl.pallas_call(
        cut_kernel,
        in_specs=[pl.BlockSpec(memory_space=pltpu.SMEM), vmem, vmem, pl.BlockSpec(memory_space=pl.ANY)],
        out_specs=[vmem] * 4,
        out_shape=[jax.ShapeDtypeStruct((SPAN, COLS), jnp.bfloat16)] * 4,
        compiler_params=SMALL,
    )(place, queries, output_gradient, after)
    return out[:2], out[2:]


def join_terms_kernel(place, mine0, mine1, theirs, dk, dv):
    head = place[2]
    for j, mine in enumerate((mine0, mine1)):
        at = pl.ds(pl.multiple_of((head * KV + j) * HEAD, HEAD), HEAD)
        there = pl.ds(pl.multiple_of(((1 - head) * KV + j) * HEAD, HEAD), HEAD)
        dk[:, at] = mine[:, :HEAD]
        dv[:, at] = mine[:, HEAD:]
        dk[:, there] = theirs[j, :, :HEAD]
        dv[:, there] = theirs[j, :, HEAD:]


def join_terms(place, mine, theirs):
    vmem = pl.BlockSpec(memory_space=pltpu.VMEM)
    out = jax.ShapeDtypeStruct((SPAN, 2 * KV * HEAD), jnp.bfloat16)
    return pl.pallas_call(
        join_terms_kernel,
        in_specs=[pl.BlockSpec(memory_space=pltpu.SMEM)] + [vmem] * 3,
        out_specs=[vmem] * 2,
        out_shape=[out] * 2,
        compiler_params=SMALL,
    )(place, *mine, theirs)


def to_partner(x):
    return lax.ppermute(x, "head", [(0, 1), (1, 0)])


def across(x):
    perm = []
    for lo in range(2):
        for y in (1, 2, 3):
            for h in range(2):
                perm.append(((lo * Y + y) * 2 + h, ((1 - lo) * Y + y) * 2 + 1 - h))
    return lax.ppermute(x, ("inner", "head"), perm)


def along_y(x, by):
    return lax.ppermute(
        x, "inner", [(lo * Y + y, lo * Y + (y + by) % Y) for lo in range(2) for y in range(Y)]
    )


def along_inner(x, by):
    return lax.ppermute(x, "inner", [(i, (i + by) % 8) for i in range(8)])


def along_outer(x, by):
    return lax.ppermute(x, "outer", [(o, (o + by) % 8) for o in range(8)])


def f32(x):
    return x.astype(jnp.float32)


def bf16(x):
    return x.astype(jnp.bfloat16)


def shards(queries, keys, values, output_gradient, span_order):
    inner, outer, head = lax.axis_index("inner"), lax.axis_index("outer"), lax.axis_index("head")
    place = jnp.stack([inner, outer, head]).astype(jnp.int32)
    y = lax.rem(inner, Y)

    def cols(x, at, width):
        return lax.dynamic_slice_in_dim(x, at, width, axis=1)

    def piece(of):
        return jnp.stack(
            [
                jnp.concatenate([cols(x, (of * KV + j) * HEAD, HEAD) for x in (keys, values)], axis=1)
                for j in range(KV)
            ]
        )

    mine, theirs = piece(head), piece(1 - head)
    near = [[mine, to_partner(theirs)]]
    other = across(theirs)
    straight = [along_inner(mine, k) for k in (1, 2, 3)]
    for k in (1, 2, 3):
        near.append([straight[k - 1], along_y(jnp.where(y + k >= Y, other, near[0][1]), k)])
    near = [half for block in near for half in block]
    far = [
        [to_partner(x) for x in two] for two in cut(place, queries, output_gradient, near[1])
    ]
    far_in = [along_outer(x, 1) for x in pack(near, far[0][0])]

    dqs, backs, sums = [], [], []
    arrived = None
    for j in range(KV):
        dq_own, dq_far, near_out, far_out = attention(
            j, span_order, place, queries, output_gradient, far[j], near, far_in[j]
        )
        dqs.append(dq_own)
        backs.append(to_partner(dq_far))
        if j:
            far_out = tie(far_out, arrived, backs[0])
        arrived = along_outer(far_out, -1)
        if j:
            near_out = tie(near_out, backs[1])
        terms = f32(near_out) + f32(arrived)
        total = terms[:256]
        for k in (1, 2, 3):
            total = total + f32(along_inner(bf16(terms[k * 256 : (k + 1) * 256]), -k))
        sums.append(total)
    theirs = to_partner(jnp.stack([bf16(s[SPAN:]) for s in sums]))
    dk, dv = join_terms(place, [bf16(s[:SPAN]) for s in sums], theirs)
    return join_rows(place, dqs, backs), dk, dv


def solution(mesh):
    rows = P(("inner", "outer", "head"), None)
    return jax.shard_map(
        shards,
        mesh=mesh,
        in_specs=(rows, rows, rows, rows, P()),
        out_specs=(rows, rows, rows),
        check_vma=False,
    )
```

```python
import functools
import math

import jax
import jax.numpy as jnp
from jax import lax
from jax.experimental import pallas as pl
from jax.experimental.pallas import tpu as pltpu
from jax.sharding import PartitionSpec as P

HEAD = 128
GROUP = 6
KV = 2
WIN = 4
SPAN = 128
NEAR, FAR = (0, 1, 2, 3), (4, 5, 6, 7)
COLS = GROUP * HEAD
Y = 4
NEG = -1e30
SCALE = 1.0 / math.sqrt(HEAD)
SCALE2 = SCALE * math.log2(math.e)
NT = (((1,), (1,)), ((), ()))
NN = (((1,), (0,)), ((), ()))
SMALL = pltpu.CompilerParams(vmem_limit_bytes=6 * 1024 * 1024)


def dot(a, b, dims):
    return lax.dot_general(a, b, dims, preferred_element_type=jnp.float32)


def attend(j, order_any, ins, p_ref, ds_ref, q_ref, do_ref, kt_ref, scratch):
    q_own, do_own, q_far, do_far = ins[:4]
    near_in, far_in = ins[4:12], ins[12:]
    e_scr, dp_scr, k_scr, v_scr, order, sem = scratch
    inner, outer, head = lax.axis_index("inner"), lax.axis_index("outer"), lax.axis_index("head")
    copy = pltpu.make_async_copy(order_any, order, sem)
    copy.start()
    for n in range(16):
        both = near_in[n][j] if n < 8 else far_in[0][n - 8]
        at_r = slice(n * SPAN, (n + 1) * SPAN)
        k_scr[at_r, :] = both[:, :HEAD]
        v_scr[at_r, :] = both[:, HEAD:]
        kt_ref[:, at_r] = both[:, :HEAD].T
    copy.wait()

    def span_of(d, o, half):
        block = lax.rem(inner + 8 - d, 8) * 8 + lax.rem(outer + 8 - o, 8)
        return order[block * 2 + (head if half == 0 else 1 - head)]

    lane = lax.broadcasted_iota(jnp.int32, (1, 256), 1)
    at = [span_of(0, 0, 0), span_of(0, 0, 1)]
    hidden = []
    for n in range(8):
        for half in range(2):
            key = span_of(n % WIN, n // WIN, half)
            first = jnp.where(key <= at[0], 0.0, -NEG)
            second = jnp.where(key <= at[1], 0.0, -NEG)
            hidden.append(jnp.where(lane < SPAN, first, second).astype(jnp.float32))
    row = lax.broadcasted_iota(jnp.int32, (256, 256), 0)
    col = lax.broadcasted_iota(jnp.int32, (256, 256), 1)
    key_pos = jnp.where(row < SPAN, at[0], at[1]) * SPAN + (row & (SPAN - 1))
    row_pos = jnp.where(col < SPAN, at[0], at[1]) * SPAN + (col & (SPAN - 1))
    own_visible = key_pos <= row_pos

    for g in range(GROUP):
        at_h = slice(g * HEAD, (g + 1) * HEAD)
        rows = slice(g * 256, (g + 1) * 256)
        q_h = jnp.concatenate([q_own[:, at_h], q_far[:, at_h]], axis=0)
        do_h = jnp.concatenate([do_own[:, at_h], do_far[:, at_h]], axis=0)
        q_ref[rows, :] = q_h
        do_ref[rows, :] = do_h
        top = jnp.full((1, 256), NEG, jnp.float32)
        tops = []
        total = jnp.zeros((8, 256), jnp.float32)
        row_dot = jnp.zeros((8, 256), jnp.float32)
        for n in range(8):
            at_r = slice(n * 256, (n + 1) * 256)
            s = dot(k_scr[at_r, :], q_h, NT)
            if n == 0:
                s = jnp.where(own_visible, s, NEG)
            dp = dot(v_scr[at_r, :], do_h, NT)
            dp_scr[at_r, :] = dp
            before = top
            for half in range(2):
                here = jnp.max(s[half * 128 : (half + 1) * 128], axis=0, keepdims=True)
                top = jnp.maximum(top, (here - hidden[2 * n + half] if n else here) * SCALE2)
            tops.append(top)
            if n:
                decay = jnp.exp2(before - top)
                total, row_dot = total * decay, row_dot * decay
            for half in range(2):
                at_e = slice(n * 256 + half * 128, n * 256 + half * 128 + 128)
                lower = top + hidden[2 * n + half] if n else top
                e = jnp.exp2(s[half * 128 : (half + 1) * 128] * SCALE2 - lower)
                e_scr[at_e, :] = e
                total = total + jnp.sum(e.reshape(16, 8, 256), axis=0)
                product = e * dp[half * 128 : (half + 1) * 128]
                row_dot = row_dot + jnp.sum(product.reshape(16, 8, 256), axis=0)
        inverse = 1.0 / jnp.sum(total, axis=0, keepdims=True)
        row_dot = jnp.sum(row_dot, axis=0, keepdims=True) * inverse
        for n in range(8):
            at_r = slice(n * 256, (n + 1) * 256)
            p = e_scr[at_r, :] * (inverse * jnp.exp2(tops[n] - top))
            ds = p * (dp_scr[at_r, :] - row_dot)
            p_ref[at_r, rows] = p.astype(jnp.bfloat16)
            ds_ref[at_r, rows] = ds.astype(jnp.bfloat16)


def terms(ns, p, ds, q, do, out):
    for i, n in enumerate(ns):
        at_r, at_o = slice(n * 256, (n + 1) * 256), slice(i * 256, (i + 1) * 256)
        out[at_o, :HEAD] = (dot(ds[at_r, :], q[...], NN) * SCALE).astype(jnp.bfloat16)
        out[at_o, HEAD:] = dot(p[at_r, :], do[...], NN).astype(jnp.bfloat16)


def row_gradient(ds, kt, dq_own, dq_far):
    for g in range(GROUP):
        dq = dot(kt[...], ds[:, g * 256 : (g + 1) * 256], NN) * SCALE
        dq = dq.T.astype(jnp.bfloat16)
        dq_own[:, g * HEAD : (g + 1) * HEAD] = dq[:SPAN]
        dq_far[:, g * HEAD : (g + 1) * HEAD] = dq[SPAN:]


def whole_kernel(j, order, *refs):
    ins, (far_out, near_out, dq_own, dq_far) = refs[:13], refs[13:17]
    p, ds, q, do, kt = refs[17:22]
    attend(j, order, ins, p, ds, q, do, kt, refs[22:])
    terms(FAR, p, ds, q, do, far_out)
    terms(NEAR, p, ds, q, do, near_out)
    row_gradient(ds, kt, dq_own, dq_far)


def early_kernel(j, order, *refs):
    (q_own, do_own, far), (far_out, p, ds, q, do, kt) = refs[:3], refs[12:18]
    ins = (q_own, do_own, far.at[0], far.at[1], *refs[3:12])
    attend(j, order, ins, p, ds, q, do, kt, refs[18:])
    terms(FAR, p, ds, q, do, far_out)


def late_kernel(p, ds, q, do, kt, near_out, dq_own, dq_far):
    terms(NEAR, p, ds, q, do, near_out)
    row_gradient(ds, kt, dq_own, dq_far)


TERMS = jax.ShapeDtypeStruct((WIN * 256, 256), jnp.bfloat16)
ROWS = jax.ShapeDtypeStruct((SPAN, COLS), jnp.bfloat16)
KEPT = (
    jax.ShapeDtypeStruct((2048, GROUP * 256), jnp.bfloat16),
    jax.ShapeDtypeStruct((2048, GROUP * 256), jnp.bfloat16),
    jax.ShapeDtypeStruct((GROUP * 256, HEAD), jnp.bfloat16),
    jax.ShapeDtypeStruct((GROUP * 256, HEAD), jnp.bfloat16),
    jax.ShapeDtypeStruct((HEAD, 2048), jnp.bfloat16),
)


def work(scores, near, rows):
    flops = 8 * 6 * 256 * 2048 * 128 * (3 * scores + near + rows)
    return pl.CostEstimate(
        flops=flops, bytes_accessed=5_000_000, transcendentals=scores * 6 * 256 * 2048
    )


def attention(j, split, order, own, far, near_in, far_in):
    free = pl.BlockSpec(memory_space=pl.ANY)
    vmem = pl.BlockSpec(memory_space=pltpu.VMEM)
    kept = [pltpu.VMEM(x.shape, x.dtype) for x in KEPT]
    out = (TERMS, *KEPT) if split else (TERMS, TERMS, ROWS, ROWS)
    return pl.pallas_call(
        functools.partial(early_kernel if split else whole_kernel, j),
        in_specs=[free] + [vmem] * (2 + len(far) + 8 + len(far_in)),
        out_specs=[vmem] * len(out),
        out_shape=out,
        scratch_shapes=([] if split else kept)
        + [
            pltpu.VMEM((2048, 256), jnp.float32),
            pltpu.VMEM((2048, 256), jnp.float32),
            pltpu.VMEM((2048, HEAD), jnp.bfloat16),
            pltpu.VMEM((2048, HEAD), jnp.bfloat16),
            pltpu.SMEM((2 * 64,), jnp.int32),
            pltpu.SemaphoreType.DMA,
        ],
        compiler_params=pltpu.CompilerParams(vmem_limit_bytes=(20 if split else 32) * 1024 * 1024),
        cost_estimate=work(1, 0 if split else 1, 0 if split else 1),
    )(order, *own, *far, *near_in, *far_in)


def rest(kept):
    vmem = pl.BlockSpec(memory_space=pltpu.VMEM)
    return pl.pallas_call(
        late_kernel,
        in_specs=[vmem] * 5,
        out_specs=[vmem] * 3,
        out_shape=(TERMS, ROWS, ROWS),
        compiler_params=pltpu.CompilerParams(vmem_limit_bytes=8 * 1024 * 1024),
        cost_estimate=pl.CostEstimate(flops=1_000_000, bytes_accessed=1_000_000, transcendentals=0),
    )(*kept)


def pack_kernel(*refs):
    halves, out = refs[:8], refs[-2:]
    for j in range(KV):
        for n in range(8):
            out[j][n] = halves[n][j]


def pack(near, *after):
    vmem = pl.BlockSpec(memory_space=pltpu.VMEM)
    one = jax.ShapeDtypeStruct((8, SPAN, 256), jnp.bfloat16)
    return pl.pallas_call(
        pack_kernel,
        in_specs=[vmem] * 8 + [pl.BlockSpec(memory_space=pl.ANY)] * len(after),
        out_specs=[vmem] * 2,
        out_shape=[one] * 2,
        compiler_params=SMALL,
    )(*near, *after)


def tie_kernel(*refs):
    del refs


def tie(x, *after):
    free = pl.BlockSpec(memory_space=pl.ANY)
    return pl.pallas_call(
        tie_kernel,
        in_specs=[free] * (1 + len(after)),
        out_specs=free,
        out_shape=jax.ShapeDtypeStruct(x.shape, x.dtype),
        input_output_aliases={0: 0},
        compiler_params=SMALL,
    )(x, *after)


def join_rows_kernel(own0, own1, back0, back1, out):
    head = lax.axis_index("head")
    for x, h, j in ((own0, head, 0), (own1, head, 1), (back0, 1 - head, 0), (back1, 1 - head, 1)):
        out[:, pl.ds(pl.multiple_of((h * KV + j) * COLS, COLS), COLS)] = x[...]


def join_rows(own, back):
    vmem = pl.BlockSpec(memory_space=pltpu.VMEM)
    return pl.pallas_call(
        join_rows_kernel,
        in_specs=[vmem] * 4,
        out_specs=vmem,
        out_shape=jax.ShapeDtypeStruct((SPAN, 2 * KV * COLS), jnp.bfloat16),
        compiler_params=SMALL,
    )(*own, *back)


def cut_kernel(queries, output_gradient, order, after, *refs):
    del after
    order_out, sems = refs[5:]
    outs = [*refs[:4], refs[4].at[0], refs[4].at[1]]
    head = lax.axis_index("head")
    copies = [pltpu.make_async_copy(order, order_out, sems.at[6])]
    for n, out in enumerate(outs):
        at, m = (head, n) if n < 4 else (1 - head, n - 2)
        at = pl.ds(pl.multiple_of((at * KV + m // 2) * COLS, COLS), COLS)
        copies.append(
            pltpu.make_async_copy((queries, output_gradient)[m % 2].at[:, at], out, sems.at[n])
        )
    for copy in copies:
        copy.start()
    for copy in copies:
        copy.wait()


def cut(queries, output_gradient, order, after):
    vmem = pl.BlockSpec(memory_space=pltpu.VMEM)
    free = pl.BlockSpec(memory_space=pl.ANY)
    out = pl.pallas_call(
        cut_kernel,
        in_specs=[free] * 4,
        out_specs=[vmem] * 6,
        out_shape=[ROWS] * 4
        + [
            jax.ShapeDtypeStruct((2, *ROWS.shape), ROWS.dtype),
            jax.ShapeDtypeStruct(order.shape, order.dtype),
        ],
        scratch_shapes=[pltpu.SemaphoreType.DMA((7,))],
        compiler_params=pltpu.CompilerParams(vmem_limit_bytes=6 * 1024 * 1024),
    )(queries, output_gradient, order, after)
    return (out[:2], out[2:4]), out[4], out[5]


def join_terms_kernel(mine0, mine1, theirs, dk, dv):
    head = lax.axis_index("head")
    for j, mine in enumerate((mine0, mine1)):
        at = pl.ds(pl.multiple_of((head * KV + j) * HEAD, HEAD), HEAD)
        there = pl.ds(pl.multiple_of(((1 - head) * KV + j) * HEAD, HEAD), HEAD)
        dk[:, at] = mine[:, :HEAD]
        dv[:, at] = mine[:, HEAD:]
        dk[:, there] = theirs[j, :, :HEAD]
        dv[:, there] = theirs[j, :, HEAD:]


def join_terms(mine, theirs):
    vmem = pl.BlockSpec(memory_space=pltpu.VMEM)
    out = jax.ShapeDtypeStruct((SPAN, 2 * KV * HEAD), jnp.bfloat16)
    return pl.pallas_call(
        join_terms_kernel,
        in_specs=[vmem] * 3,
        out_specs=[vmem] * 2,
        out_shape=[out] * 2,
        compiler_params=SMALL,
    )(*mine, theirs)


def to_partner(x):
    return lax.ppermute(x, "head", [(0, 1), (1, 0)])


def across(x):
    perm = []
    for lo in range(2):
        for y in (1, 2, 3):
            for h in range(2):
                perm.append(((lo * Y + y) * 2 + h, ((1 - lo) * Y + y) * 2 + 1 - h))
    return lax.ppermute(x, ("inner", "head"), perm)


def along_y(x, by):
    return lax.ppermute(
        x, "inner", [(lo * Y + y, lo * Y + (y + by) % Y) for lo in range(2) for y in range(Y)]
    )


def along_inner(x, by):
    return lax.ppermute(x, "inner", [(i, (i + by) % 8) for i in range(8)])


def along_outer(x, by):
    return lax.ppermute(x, "outer", [(o, (o + by) % 8) for o in range(8)])


def f32(x):
    return x.astype(jnp.float32)


def bf16(x):
    return x.astype(jnp.bfloat16)


def send_terms(near_out, arrived):
    total = f32(near_out) + f32(arrived)
    return total[:256], [along_inner(bf16(total[k * 256 : (k + 1) * 256]), -k) for k in (1, 2, 3)]


def shards(queries, keys, values, output_gradient, span_order):
    inner, head = lax.axis_index("inner"), lax.axis_index("head")
    y = lax.rem(inner, Y)

    def cols(x, at, width):
        return lax.dynamic_slice_in_dim(x, at, width, axis=1)

    def piece(of):
        return jnp.stack(
            [
                jnp.concatenate([cols(x, (of * KV + j) * HEAD, HEAD) for x in (keys, values)], axis=1)
                for j in range(KV)
            ]
        )

    mine, theirs = piece(head), piece(1 - head)
    near = [[mine, to_partner(theirs)]]
    other = across(theirs)
    straight = [along_inner(mine, k) for k in (1, 2, 3)]
    for k in (1, 2, 3):
        near.append([straight[k - 1], along_y(jnp.where(y + k >= Y, other, near[0][1]), k)])
    near = [half for block in near for half in block]
    own, far, order = cut(queries, output_gradient, span_order, near[3])
    first_far = [cols(x, (1 - head) * KV * COLS, COLS) for x in (queries, output_gradient)]
    far = [[to_partner(x) for x in first_far], [to_partner(far)]]
    far_in = [(along_outer(x, 1),) for x in pack(near, far[0][0])]
    far_out0, near_out0, dq_own0, dq_far0 = attention(0, False, order, own[0], far[0], near, far_in[0])
    back0 = to_partner(dq_far0)
    arrived0 = along_outer(far_out0, -1)
    far_out1, *kept = attention(1, True, order, own[1], far[1], near, far_in[1])
    arrived1 = along_outer(tie(far_out1, arrived0), -1)
    total0, moved0 = send_terms(tie(near_out0, back0), arrived0)
    near_out1, dq_own1, dq_far1 = rest(kept)
    back1 = to_partner(dq_far1)
    total1, moved1 = send_terms(tie(near_out1, *moved0), arrived1)
    sums = [total0, total1]
    for n, moved in enumerate((moved0, moved1)):
        for x in moved:
            sums[n] = sums[n] + f32(x)
    theirs = to_partner(jnp.stack([bf16(s[SPAN:]) for s in sums]))
    dk, dv = join_terms([bf16(s[:SPAN]) for s in sums], theirs)
    return join_rows((dq_own0, dq_own1), (back0, back1)), dk, dv


def solution(mesh):
    rows = P(("inner", "outer", "head"), None)
    return jax.shard_map(
        shards,
        mesh=mesh,
        in_specs=(rows, rows, rows, rows, P()),
        out_specs=(rows, rows, rows),
        check_vma=False,
    )
```

```python
import functools
import math

import jax
import jax.numpy as jnp
from jax import lax
from jax.experimental import pallas as pl
from jax.experimental.pallas import tpu as pltpu
from jax.sharding import PartitionSpec as P

HEAD = 128
GROUP = 6
KV = 2
WIN = 4
SPAN = 128
NEAR, FAR = (0, 1, 2, 3), (4, 5, 6, 7)
COLS = GROUP * HEAD
Y = 4
NEG = -1e30
SCALE = 1.0 / math.sqrt(HEAD)
SCALE2 = SCALE * math.log2(math.e)
NT = (((1,), (1,)), ((), ()))
NN = (((1,), (0,)), ((), ()))
SMALL = pltpu.CompilerParams(vmem_limit_bytes=6 * 1024 * 1024)


def dot(a, b, dims):
    return lax.dot_general(a, b, dims, preferred_element_type=jnp.float32)


def attend(j, order_any, ins, p_ref, ds_ref, q_ref, do_ref, kt_ref, scratch):
    q_own, do_own, q_far, do_far = ins[:4]
    near_in, far_in = ins[4:12], ins[12:]
    e_scr, dp_scr, k_scr, v_scr, order, sem = scratch
    inner, outer, head = lax.axis_index("inner"), lax.axis_index("outer"), lax.axis_index("head")
    copy = pltpu.make_async_copy(order_any, order, sem)
    copy.start()
    for n in range(16):
        both = near_in[n][j] if n < 8 else far_in[0][n - 8]
        at_r = slice(n * SPAN, (n + 1) * SPAN)
        k_scr[at_r, :] = both[:, :HEAD]
        v_scr[at_r, :] = both[:, HEAD:]
        kt_ref[:, at_r] = both[:, :HEAD].T
    copy.wait()

    def span_of(d, o, half):
        block = lax.rem(inner + 8 - d, 8) * 8 + lax.rem(outer + 8 - o, 8)
        return order[block * 2 + (head if half == 0 else 1 - head)]

    lane = lax.broadcasted_iota(jnp.int32, (1, 256), 1)
    at = [span_of(0, 0, 0), span_of(0, 0, 1)]
    hidden = []
    for n in range(8):
        for half in range(2):
            key = span_of(n % WIN, n // WIN, half)
            first = jnp.where(key <= at[0], 0.0, -NEG)
            second = jnp.where(key <= at[1], 0.0, -NEG)
            hidden.append(jnp.where(lane < SPAN, first, second).astype(jnp.float32))
    row = lax.broadcasted_iota(jnp.int32, (256, 256), 0)
    col = lax.broadcasted_iota(jnp.int32, (256, 256), 1)
    key_pos = jnp.where(row < SPAN, at[0], at[1]) * SPAN + (row & (SPAN - 1))
    row_pos = jnp.where(col < SPAN, at[0], at[1]) * SPAN + (col & (SPAN - 1))
    own_visible = key_pos <= row_pos

    for g in range(GROUP):
        at_h = slice(g * HEAD, (g + 1) * HEAD)
        rows = slice(g * 256, (g + 1) * 256)
        q_h = jnp.concatenate([q_own[:, at_h], q_far[:, at_h]], axis=0)
        do_h = jnp.concatenate([do_own[:, at_h], do_far[:, at_h]], axis=0)
        q_ref[rows, :] = q_h
        do_ref[rows, :] = do_h
        top = jnp.full((1, 256), NEG, jnp.float32)
        tops = []
        total = jnp.zeros((8, 256), jnp.float32)
        row_dot = jnp.zeros((8, 256), jnp.float32)
        for n in range(8):
            at_r = slice(n * 256, (n + 1) * 256)
            s = dot(k_scr[at_r, :], q_h, NT)
            if n == 0:
                s = jnp.where(own_visible, s, NEG)
            dp = dot(v_scr[at_r, :], do_h, NT)
            dp_scr[at_r, :] = dp
            before = top
            for half in range(2):
                here = jnp.max(s[half * 128 : (half + 1) * 128], axis=0, keepdims=True)
                top = jnp.maximum(top, (here - hidden[2 * n + half] if n else here) * SCALE2)
            tops.append(top)
            if n:
                decay = jnp.exp2(before - top)
                total, row_dot = total * decay, row_dot * decay
            for half in range(2):
                at_e = slice(n * 256 + half * 128, n * 256 + half * 128 + 128)
                lower = top + hidden[2 * n + half] if n else top
                e = jnp.exp2(s[half * 128 : (half + 1) * 128] * SCALE2 - lower)
                e_scr[at_e, :] = e
                total = total + jnp.sum(e.reshape(16, 8, 256), axis=0)
                product = e * dp[half * 128 : (half + 1) * 128]
                row_dot = row_dot + jnp.sum(product.reshape(16, 8, 256), axis=0)
        inverse = 1.0 / jnp.sum(total, axis=0, keepdims=True)
        row_dot = jnp.sum(row_dot, axis=0, keepdims=True) * inverse
        for n in range(8):
            at_r = slice(n * 256, (n + 1) * 256)
            p = e_scr[at_r, :] * (inverse * jnp.exp2(tops[n] - top))
            ds = p * (dp_scr[at_r, :] - row_dot)
            p_ref[at_r, rows] = p.astype(jnp.bfloat16)
            ds_ref[at_r, rows] = ds.astype(jnp.bfloat16)


def terms(ns, p, ds, q, do, out):
    for i, n in enumerate(ns):
        at_r, at_o = slice(n * 256, (n + 1) * 256), slice(i * 256, (i + 1) * 256)
        out[at_o, :HEAD] = (dot(ds[at_r, :], q[...], NN) * SCALE).astype(jnp.bfloat16)
        out[at_o, HEAD:] = dot(p[at_r, :], do[...], NN).astype(jnp.bfloat16)


def row_gradient(ds, kt, dq_own, dq_far):
    for g in range(GROUP):
        dq = dot(kt[...], ds[:, g * 256 : (g + 1) * 256], NN) * SCALE
        dq = dq.T.astype(jnp.bfloat16)
        dq_own[:, g * HEAD : (g + 1) * HEAD] = dq[:SPAN]
        dq_far[:, g * HEAD : (g + 1) * HEAD] = dq[SPAN:]


def whole_kernel(j, order, *refs):
    ins, (far_out, near_out, dq_own, dq_far) = refs[:13], refs[13:17]
    p, ds, q, do, kt = refs[17:22]
    attend(j, order, ins, p, ds, q, do, kt, refs[22:])
    terms(FAR, p, ds, q, do, far_out)
    terms(NEAR, p, ds, q, do, near_out)
    row_gradient(ds, kt, dq_own, dq_far)


def early_kernel(j, order, *refs):
    (q_own, do_own, far), (far_out, p, ds, q, do, kt) = refs[:3], refs[12:18]
    ins = (q_own, do_own, far.at[0], far.at[1], *refs[3:12])
    attend(j, order, ins, p, ds, q, do, kt, refs[18:])
    terms(FAR, p, ds, q, do, far_out)


def late_kernel(p, ds, q, do, kt, near_out, dq_own, dq_far):
    terms(NEAR, p, ds, q, do, near_out)
    row_gradient(ds, kt, dq_own, dq_far)


TERMS = jax.ShapeDtypeStruct((WIN * 256, 256), jnp.bfloat16)
ROWS = jax.ShapeDtypeStruct((SPAN, COLS), jnp.bfloat16)
KEPT = (
    jax.ShapeDtypeStruct((2048, GROUP * 256), jnp.bfloat16),
    jax.ShapeDtypeStruct((2048, GROUP * 256), jnp.bfloat16),
    jax.ShapeDtypeStruct((GROUP * 256, HEAD), jnp.bfloat16),
    jax.ShapeDtypeStruct((GROUP * 256, HEAD), jnp.bfloat16),
    jax.ShapeDtypeStruct((HEAD, 2048), jnp.bfloat16),
)


def work(scores, near, rows):
    flops = 8 * 6 * 256 * 2048 * 128 * (3 * scores + near + rows)
    return pl.CostEstimate(
        flops=flops, bytes_accessed=5_000_000, transcendentals=scores * 6 * 256 * 2048
    )


def attention(j, split, order, own, far, near_in, far_in):
    free = pl.BlockSpec(memory_space=pl.ANY)
    vmem = pl.BlockSpec(memory_space=pltpu.VMEM)
    kept = [pltpu.VMEM(x.shape, x.dtype) for x in KEPT]
    out = (TERMS, *KEPT) if split else (TERMS, TERMS, ROWS, ROWS)
    return pl.pallas_call(
        functools.partial(early_kernel if split else whole_kernel, j),
        in_specs=[free] + [vmem] * (2 + len(far) + 8 + len(far_in)),
        out_specs=[vmem] * len(out),
        out_shape=out,
        scratch_shapes=([] if split else kept)
        + [
            pltpu.VMEM((2048, 256), jnp.float32),
            pltpu.VMEM((2048, 256), jnp.float32),
            pltpu.VMEM((2048, HEAD), jnp.bfloat16),
            pltpu.VMEM((2048, HEAD), jnp.bfloat16),
            pltpu.SMEM((2 * 64,), jnp.int32),
            pltpu.SemaphoreType.DMA,
        ],
        compiler_params=pltpu.CompilerParams(vmem_limit_bytes=(20 if split else 32) * 1024 * 1024),
        cost_estimate=work(1, 0 if split else 1, 0 if split else 1),
    )(order, *own, *far, *near_in, *far_in)


def rest(kept):
    vmem = pl.BlockSpec(memory_space=pltpu.VMEM)
    return pl.pallas_call(
        late_kernel,
        in_specs=[vmem] * 5,
        out_specs=[vmem] * 3,
        out_shape=(TERMS, ROWS, ROWS),
        compiler_params=pltpu.CompilerParams(vmem_limit_bytes=8 * 1024 * 1024),
        cost_estimate=pl.CostEstimate(flops=1_000_000, bytes_accessed=1_000_000, transcendentals=0),
    )(*kept)


def pack_kernel(*refs):
    halves, out = refs[:8], refs[-2:]
    for j in range(KV):
        for n in range(8):
            out[j][n] = halves[n][j]


def pack(near, *after):
    vmem = pl.BlockSpec(memory_space=pltpu.VMEM)
    one = jax.ShapeDtypeStruct((8, SPAN, 256), jnp.bfloat16)
    return pl.pallas_call(
        pack_kernel,
        in_specs=[vmem] * 8 + [pl.BlockSpec(memory_space=pl.ANY)] * len(after),
        out_specs=[vmem] * 2,
        out_shape=[one] * 2,
        compiler_params=SMALL,
    )(*near, *after)


def tie_kernel(*refs):
    del refs


def tie(x, *after):
    free = pl.BlockSpec(memory_space=pl.ANY)
    return pl.pallas_call(
        tie_kernel,
        in_specs=[free] * (1 + len(after)),
        out_specs=free,
        out_shape=jax.ShapeDtypeStruct(x.shape, x.dtype),
        input_output_aliases={0: 0},
        compiler_params=SMALL,
    )(x, *after)


def join_rows_kernel(own0, own1, back0, back1, out):
    head = lax.axis_index("head")
    for x, h, j in ((own0, head, 0), (own1, head, 1), (back0, 1 - head, 0), (back1, 1 - head, 1)):
        out[:, pl.ds(pl.multiple_of((h * KV + j) * COLS, COLS), COLS)] = x[...]


def join_rows(own, back):
    vmem = pl.BlockSpec(memory_space=pltpu.VMEM)
    return pl.pallas_call(
        join_rows_kernel,
        in_specs=[vmem] * 4,
        out_specs=vmem,
        out_shape=jax.ShapeDtypeStruct((SPAN, 2 * KV * COLS), jnp.bfloat16),
        compiler_params=SMALL,
    )(*own, *back)


def cut_kernel(queries, output_gradient, order, after, *refs):
    del after
    order_out, sems = refs[5:]
    outs = [*refs[:4], refs[4].at[0], refs[4].at[1]]
    head = lax.axis_index("head")
    copies = [pltpu.make_async_copy(order, order_out, sems.at[6])]
    for n, out in enumerate(outs):
        at, m = (head, n) if n < 4 else (1 - head, n - 2)
        at = pl.ds(pl.multiple_of((at * KV + m // 2) * COLS, COLS), COLS)
        copies.append(
            pltpu.make_async_copy((queries, output_gradient)[m % 2].at[:, at], out, sems.at[n])
        )
    for copy in copies:
        copy.start()
    for copy in copies:
        copy.wait()


def cut(queries, output_gradient, order, after):
    vmem = pl.BlockSpec(memory_space=pltpu.VMEM)
    free = pl.BlockSpec(memory_space=pl.ANY)
    out = pl.pallas_call(
        cut_kernel,
        in_specs=[free] * 4,
        out_specs=[vmem] * 6,
        out_shape=[ROWS] * 4
        + [
            jax.ShapeDtypeStruct((2, *ROWS.shape), ROWS.dtype),
            jax.ShapeDtypeStruct(order.shape, order.dtype),
        ],
        scratch_shapes=[pltpu.SemaphoreType.DMA((7,))],
        compiler_params=pltpu.CompilerParams(vmem_limit_bytes=6 * 1024 * 1024),
    )(queries, output_gradient, order, after)
    return (out[:2], out[2:4]), out[4], out[5]


def join_terms_kernel(mine0, mine1, theirs, dk, dv):
    head = lax.axis_index("head")
    for j, mine in enumerate((mine0, mine1)):
        at = pl.ds(pl.multiple_of((head * KV + j) * HEAD, HEAD), HEAD)
        there = pl.ds(pl.multiple_of(((1 - head) * KV + j) * HEAD, HEAD), HEAD)
        dk[:, at] = mine[:, :HEAD]
        dv[:, at] = mine[:, HEAD:]
        dk[:, there] = theirs[j, :, :HEAD]
        dv[:, there] = theirs[j, :, HEAD:]


def join_terms(mine, theirs):
    vmem = pl.BlockSpec(memory_space=pltpu.VMEM)
    out = jax.ShapeDtypeStruct((SPAN, 2 * KV * HEAD), jnp.bfloat16)
    return pl.pallas_call(
        join_terms_kernel,
        in_specs=[vmem] * 3,
        out_specs=[vmem] * 2,
        out_shape=[out] * 2,
        compiler_params=SMALL,
    )(*mine, theirs)


def to_partner(x):
    return lax.ppermute(x, "head", [(0, 1), (1, 0)])


def across(x):
    perm = []
    for lo in range(2):
        for y in (1, 2, 3):
            for h in range(2):
                perm.append(((lo * Y + y) * 2 + h, ((1 - lo) * Y + y) * 2 + 1 - h))
    return lax.ppermute(x, ("inner", "head"), perm)


def along_y(x, by):
    return lax.ppermute(
        x, "inner", [(lo * Y + y, lo * Y + (y + by) % Y) for lo in range(2) for y in range(Y)]
    )


def along_inner(x, by):
    return lax.ppermute(x, "inner", [(i, (i + by) % 8) for i in range(8)])


def along_outer(x, by):
    return lax.ppermute(x, "outer", [(o, (o + by) % 8) for o in range(8)])


def f32(x):
    return x.astype(jnp.float32)


def bf16(x):
    return x.astype(jnp.bfloat16)


def send_terms(near_out, arrived):
    total = f32(near_out) + f32(arrived)
    return total[:256], [along_inner(bf16(total[k * 256 : (k + 1) * 256]), -k) for k in (1, 2, 3)]


def shards(queries, keys, values, output_gradient, span_order):
    inner, head = lax.axis_index("inner"), lax.axis_index("head")
    y = lax.rem(inner, Y)

    def cols(x, at, width):
        return lax.dynamic_slice_in_dim(x, at, width, axis=1)

    def piece(of):
        return jnp.stack(
            [
                jnp.concatenate([cols(x, (of * KV + j) * HEAD, HEAD) for x in (keys, values)], axis=1)
                for j in range(KV)
            ]
        )

    mine, theirs = piece(head), piece(1 - head)
    near = [[mine, to_partner(theirs)]]
    other = across(theirs)
    straight = [along_inner(mine, k) for k in (1, 2, 3)]
    for k in (1, 2, 3):
        near.append([straight[k - 1], along_y(jnp.where(y + k >= Y, other, near[0][1]), k)])
    near = [half for block in near for half in block]
    own, far, order = cut(queries, output_gradient, span_order, near[3])
    first_far = [cols(x, (1 - head) * KV * COLS, COLS) for x in (queries, output_gradient)]
    far = [[to_partner(x) for x in first_far], [to_partner(far)]]
    far_in = [(along_outer(x, 1),) for x in pack(near, far[0][0], first_far[1])]
    far_out0, near_out0, dq_own0, dq_far0 = attention(0, False, order, own[0], far[0], near, far_in[0])
    back0 = to_partner(dq_far0)
    arrived0 = along_outer(far_out0, -1)
    far_out1, *kept = attention(1, True, order, own[1], far[1], near, far_in[1])
    arrived1 = along_outer(tie(far_out1, arrived0), -1)
    total0, moved0 = send_terms(tie(near_out0, back0), arrived0)
    near_out1, dq_own1, dq_far1 = rest(kept)
    total1, moved1 = send_terms(tie(near_out1, *moved0), arrived1)
    back1 = to_partner(tie(dq_far1, moved1[0]))
    sums = [total0, total1]
    for n, moved in enumerate((moved0, moved1)):
        for x in moved:
            sums[n] = sums[n] + f32(x)
    theirs = to_partner(jnp.stack([bf16(s[SPAN:]) for s in sums]))
    dk, dv = join_terms([bf16(s[:SPAN]) for s in sums], theirs)
    return join_rows((dq_own0, dq_own1), (back0, back1)), dk, dv


def solution(mesh):
    rows = P(("inner", "outer", "head"), None)
    return jax.shard_map(
        shards,
        mesh=mesh,
        in_specs=(rows, rows, rows, rows, P()),
        out_specs=(rows, rows, rows),
        check_vma=False,
    )
```

```python
import functools
import math

import jax
import jax.numpy as jnp
from jax import lax
from jax.experimental import pallas as pl
from jax.experimental.pallas import tpu as pltpu
from jax.sharding import PartitionSpec as P

HEAD = 128
GROUP = 6
KV = 2
WIN = 4
SPAN = 128
NEAR, FAR = (0, 1, 2, 3), (4, 5, 6, 7)
COLS = GROUP * HEAD
Y = 4
NEG = -1e30
SCALE = 1.0 / math.sqrt(HEAD)
SCALE2 = SCALE * math.log2(math.e)
NT = (((1,), (1,)), ((), ()))
NN = (((1,), (0,)), ((), ()))
SMALL = pltpu.CompilerParams(vmem_limit_bytes=6 * 1024 * 1024)


def dot(a, b, dims):
    return lax.dot_general(a, b, dims, preferred_element_type=jnp.float32)


def attend(j, order_any, ins, p_ref, ds_ref, q_ref, do_ref, kt_ref, scratch):
    q_own, do_own, q_far, do_far = ins[:4]
    near_in, far_in = ins[4:12], ins[12:]
    e_scr, dp_scr, k_scr, v_scr, order, sem = scratch
    inner, outer, head = lax.axis_index("inner"), lax.axis_index("outer"), lax.axis_index("head")
    copy = pltpu.make_async_copy(order_any, order, sem)
    copy.start()
    for n in range(16):
        both = near_in[n][j] if n < 8 else far_in[0][n - 8]
        at_r = slice(n * SPAN, (n + 1) * SPAN)
        k_scr[at_r, :] = both[:, :HEAD]
        v_scr[at_r, :] = both[:, HEAD:]
        kt_ref[:, at_r] = both[:, :HEAD].T
    copy.wait()

    def span_of(d, o, half):
        block = lax.rem(inner + 8 - d, 8) * 8 + lax.rem(outer + 8 - o, 8)
        return order[block * 2 + (head if half == 0 else 1 - head)]

    lane = lax.broadcasted_iota(jnp.int32, (1, 256), 1)
    at = [span_of(0, 0, 0), span_of(0, 0, 1)]
    hidden = []
    for n in range(8):
        for half in range(2):
            key = span_of(n % WIN, n // WIN, half)
            first = jnp.where(key <= at[0], 0.0, -NEG)
            second = jnp.where(key <= at[1], 0.0, -NEG)
            hidden.append(jnp.where(lane < SPAN, first, second).astype(jnp.float32))
    row = lax.broadcasted_iota(jnp.int32, (256, 256), 0)
    col = lax.broadcasted_iota(jnp.int32, (256, 256), 1)
    key_pos = jnp.where(row < SPAN, at[0], at[1]) * SPAN + (row & (SPAN - 1))
    row_pos = jnp.where(col < SPAN, at[0], at[1]) * SPAN + (col & (SPAN - 1))
    own_visible = key_pos <= row_pos

    for g in range(GROUP):
        at_h = slice(g * HEAD, (g + 1) * HEAD)
        rows = slice(g * 256, (g + 1) * 256)
        q_h = jnp.concatenate([q_own[:, at_h], q_far[:, at_h]], axis=0)
        do_h = jnp.concatenate([do_own[:, at_h], do_far[:, at_h]], axis=0)
        q_ref[rows, :] = q_h
        do_ref[rows, :] = do_h
        top = jnp.full((1, 256), NEG, jnp.float32)
        tops = []
        total = jnp.zeros((8, 256), jnp.float32)
        row_dot = jnp.zeros((8, 256), jnp.float32)
        for n in range(8):
            at_r = slice(n * 256, (n + 1) * 256)
            s = dot(k_scr[at_r, :], q_h, NT)
            if n == 0:
                s = jnp.where(own_visible, s, NEG)
            dp = dot(v_scr[at_r, :], do_h, NT)
            dp_scr[at_r, :] = dp
            before = top
            for half in range(2):
                here = jnp.max(s[half * 128 : (half + 1) * 128], axis=0, keepdims=True)
                top = jnp.maximum(top, (here - hidden[2 * n + half] if n else here) * SCALE2)
            tops.append(top)
            if n:
                decay = jnp.exp2(before - top)
                total, row_dot = total * decay, row_dot * decay
            for half in range(2):
                at_e = slice(n * 256 + half * 128, n * 256 + half * 128 + 128)
                lower = top + hidden[2 * n + half] if n else top
                e = jnp.exp2(s[half * 128 : (half + 1) * 128] * SCALE2 - lower)
                e_scr[at_e, :] = e
                total = total + jnp.sum(e.reshape(16, 8, 256), axis=0)
                product = e * dp[half * 128 : (half + 1) * 128]
                row_dot = row_dot + jnp.sum(product.reshape(16, 8, 256), axis=0)
        inverse = 1.0 / jnp.sum(total, axis=0, keepdims=True)
        row_dot = jnp.sum(row_dot, axis=0, keepdims=True) * inverse
        for n in range(8):
            at_r = slice(n * 256, (n + 1) * 256)
            p = e_scr[at_r, :] * (inverse * jnp.exp2(tops[n] - top))
            ds = p * (dp_scr[at_r, :] - row_dot)
            p_ref[at_r, rows] = p.astype(jnp.bfloat16)
            ds_ref[at_r, rows] = ds.astype(jnp.bfloat16)


def terms(ns, p, ds, q, do, out):
    for i, n in enumerate(ns):
        at_r, at_o = slice(n * 256, (n + 1) * 256), slice(i * 256, (i + 1) * 256)
        out[at_o, :HEAD] = (dot(ds[at_r, :], q[...], NN) * SCALE).astype(jnp.bfloat16)
        out[at_o, HEAD:] = dot(p[at_r, :], do[...], NN).astype(jnp.bfloat16)


def row_gradient(ds, kt, dq_own, dq_far):
    for g in range(GROUP):
        dq = dot(kt[...], ds[:, g * 256 : (g + 1) * 256], NN) * SCALE
        dq = dq.T.astype(jnp.bfloat16)
        dq_own[:, g * HEAD : (g + 1) * HEAD] = dq[:SPAN]
        dq_far[:, g * HEAD : (g + 1) * HEAD] = dq[SPAN:]


def whole_kernel(j, order, *refs):
    ins, (far_out, near_out, dq_own, dq_far) = refs[:13], refs[13:17]
    p, ds, q, do, kt = refs[17:22]
    attend(j, order, ins, p, ds, q, do, kt, refs[22:])
    terms(FAR, p, ds, q, do, far_out)
    terms(NEAR, p, ds, q, do, near_out)
    row_gradient(ds, kt, dq_own, dq_far)


def early_kernel(j, order, *refs):
    (q_own, do_own, far), (far_out, p, ds, q, do, kt) = refs[:3], refs[12:18]
    ins = (q_own, do_own, far.at[0], far.at[1], *refs[3:12])
    attend(j, order, ins, p, ds, q, do, kt, refs[18:])
    terms(FAR, p, ds, q, do, far_out)


def late_kernel(p, ds, q, do, kt, near_out, dq_own, dq_far):
    terms(NEAR, p, ds, q, do, near_out)
    row_gradient(ds, kt, dq_own, dq_far)


TERMS = jax.ShapeDtypeStruct((WIN * 256, 256), jnp.bfloat16)
ROWS = jax.ShapeDtypeStruct((SPAN, COLS), jnp.bfloat16)
KEPT = (
    jax.ShapeDtypeStruct((2048, GROUP * 256), jnp.bfloat16),
    jax.ShapeDtypeStruct((2048, GROUP * 256), jnp.bfloat16),
    jax.ShapeDtypeStruct((GROUP * 256, HEAD), jnp.bfloat16),
    jax.ShapeDtypeStruct((GROUP * 256, HEAD), jnp.bfloat16),
    jax.ShapeDtypeStruct((HEAD, 2048), jnp.bfloat16),
)


def work(scores, near, rows):
    flops = 8 * 6 * 256 * 2048 * 128 * (3 * scores + near + rows)
    return pl.CostEstimate(
        flops=flops, bytes_accessed=5_000_000, transcendentals=scores * 6 * 256 * 2048
    )


def attention(j, split, order, own, far, near_in, far_in):
    free = pl.BlockSpec(memory_space=pl.ANY)
    vmem = pl.BlockSpec(memory_space=pltpu.VMEM)
    kept = [pltpu.VMEM(x.shape, x.dtype) for x in KEPT]
    out = (TERMS, *KEPT) if split else (TERMS, TERMS, ROWS, ROWS)
    return pl.pallas_call(
        functools.partial(early_kernel if split else whole_kernel, j),
        in_specs=[free] + [vmem] * (2 + len(far) + 8 + len(far_in)),
        out_specs=[vmem] * len(out),
        out_shape=out,
        scratch_shapes=([] if split else kept)
        + [
            pltpu.VMEM((2048, 256), jnp.float32),
            pltpu.VMEM((2048, 256), jnp.float32),
            pltpu.VMEM((2048, HEAD), jnp.bfloat16),
            pltpu.VMEM((2048, HEAD), jnp.bfloat16),
            pltpu.SMEM((2 * 64,), jnp.int32),
            pltpu.SemaphoreType.DMA,
        ],
        compiler_params=pltpu.CompilerParams(vmem_limit_bytes=(20 if split else 32) * 1024 * 1024),
        cost_estimate=work(1, 0 if split else 1, 0 if split else 1),
    )(order, *own, *far, *near_in, *far_in)


def rest(kept):
    vmem = pl.BlockSpec(memory_space=pltpu.VMEM)
    return pl.pallas_call(
        late_kernel,
        in_specs=[vmem] * 5,
        out_specs=[vmem] * 3,
        out_shape=(TERMS, ROWS, ROWS),
        compiler_params=pltpu.CompilerParams(vmem_limit_bytes=8 * 1024 * 1024),
        cost_estimate=pl.CostEstimate(flops=1_000_000, bytes_accessed=1_000_000, transcendentals=0),
    )(*kept)


def pack_kernel(*refs):
    halves, out = refs[:8], refs[-2:]
    for j in range(KV):
        for n in range(8):
            out[j][n] = halves[n][j]


def pack(near, *after):
    vmem = pl.BlockSpec(memory_space=pltpu.VMEM)
    one = jax.ShapeDtypeStruct((8, SPAN, 256), jnp.bfloat16)
    return pl.pallas_call(
        pack_kernel,
        in_specs=[vmem] * 8 + [pl.BlockSpec(memory_space=pl.ANY)] * len(after),
        out_specs=[vmem] * 2,
        out_shape=[one] * 2,
        compiler_params=SMALL,
    )(*near, *after)


def tie_kernel(*refs):
    del refs


def tie(x, *after):
    free = pl.BlockSpec(memory_space=pl.ANY)
    return pl.pallas_call(
        tie_kernel,
        in_specs=[free] * (1 + len(after)),
        out_specs=free,
        out_shape=jax.ShapeDtypeStruct(x.shape, x.dtype),
        input_output_aliases={0: 0},
        compiler_params=SMALL,
    )(x, *after)


def join_rows_kernel(own0, own1, back0, back1, out):
    head = lax.axis_index("head")
    for x, h, j in ((own0, head, 0), (own1, head, 1), (back0, 1 - head, 0), (back1, 1 - head, 1)):
        out[:, pl.ds(pl.multiple_of((h * KV + j) * COLS, COLS), COLS)] = x[...]


def join_rows(own, back):
    vmem = pl.BlockSpec(memory_space=pltpu.VMEM)
    return pl.pallas_call(
        join_rows_kernel,
        in_specs=[vmem] * 4,
        out_specs=vmem,
        out_shape=jax.ShapeDtypeStruct((SPAN, 2 * KV * COLS), jnp.bfloat16),
        compiler_params=SMALL,
    )(*own, *back)


def cut_kernel(queries, output_gradient, order, after, *refs):
    del after
    order_out, sems = refs[5:]
    outs = [*refs[:4], refs[4].at[0], refs[4].at[1]]
    head = lax.axis_index("head")
    copies = [pltpu.make_async_copy(order, order_out, sems.at[6])]
    for n, out in enumerate(outs):
        at, m = (head, n) if n < 4 else (1 - head, n - 2)
        at = pl.ds(pl.multiple_of((at * KV + m // 2) * COLS, COLS), COLS)
        copies.append(
            pltpu.make_async_copy((queries, output_gradient)[m % 2].at[:, at], out, sems.at[n])
        )
    for copy in copies:
        copy.start()
    for copy in copies:
        copy.wait()


def cut(queries, output_gradient, order, after):
    vmem = pl.BlockSpec(memory_space=pltpu.VMEM)
    free = pl.BlockSpec(memory_space=pl.ANY)
    out = pl.pallas_call(
        cut_kernel,
        in_specs=[free] * 4,
        out_specs=[vmem] * 6,
        out_shape=[ROWS] * 4
        + [
            jax.ShapeDtypeStruct((2, *ROWS.shape), ROWS.dtype),
            jax.ShapeDtypeStruct(order.shape, order.dtype),
        ],
        scratch_shapes=[pltpu.SemaphoreType.DMA((7,))],
        compiler_params=pltpu.CompilerParams(vmem_limit_bytes=6 * 1024 * 1024),
    )(queries, output_gradient, order, after)
    return (out[:2], out[2:4]), out[4], out[5]


def join_terms_kernel(mine0, mine1, theirs, dk, dv):
    head = lax.axis_index("head")
    for j, mine in enumerate((mine0, mine1)):
        at = pl.ds(pl.multiple_of((head * KV + j) * HEAD, HEAD), HEAD)
        there = pl.ds(pl.multiple_of(((1 - head) * KV + j) * HEAD, HEAD), HEAD)
        dk[:, at] = mine[:, :HEAD]
        dv[:, at] = mine[:, HEAD:]
        dk[:, there] = theirs[j, :, :HEAD]
        dv[:, there] = theirs[j, :, HEAD:]


def join_terms(mine, theirs):
    vmem = pl.BlockSpec(memory_space=pltpu.VMEM)
    out = jax.ShapeDtypeStruct((SPAN, 2 * KV * HEAD), jnp.bfloat16)
    return pl.pallas_call(
        join_terms_kernel,
        in_specs=[vmem] * 3,
        out_specs=[vmem] * 2,
        out_shape=[out] * 2,
        compiler_params=SMALL,
    )(*mine, theirs)


def to_partner(x):
    return lax.ppermute(x, "head", [(0, 1), (1, 0)])


def across(x):
    perm = []
    for lo in range(2):
        for y in (1, 2, 3):
            for h in range(2):
                perm.append(((lo * Y + y) * 2 + h, ((1 - lo) * Y + y) * 2 + 1 - h))
    return lax.ppermute(x, ("inner", "head"), perm)


def along_y(x, by):
    return lax.ppermute(
        x, "inner", [(lo * Y + y, lo * Y + (y + by) % Y) for lo in range(2) for y in range(Y)]
    )


def along_inner(x, by):
    return lax.ppermute(x, "inner", [(i, (i + by) % 8) for i in range(8)])


def along_outer(x, by):
    return lax.ppermute(x, "outer", [(o, (o + by) % 8) for o in range(8)])


def f32(x):
    return x.astype(jnp.float32)


def bf16(x):
    return x.astype(jnp.bfloat16)


def send_terms(near_out, arrived):
    total = f32(near_out) + f32(arrived)
    return total[:256], [along_inner(bf16(total[k * 256 : (k + 1) * 256]), -k) for k in (1, 2, 3)]


def shards(queries, keys, values, output_gradient, span_order):
    inner, head = lax.axis_index("inner"), lax.axis_index("head")
    y = lax.rem(inner, Y)

    def cols(x, at, width):
        return lax.dynamic_slice_in_dim(x, at, width, axis=1)

    def piece(of):
        return jnp.stack(
            [
                jnp.concatenate([cols(x, (of * KV + j) * HEAD, HEAD) for x in (keys, values)], axis=1)
                for j in range(KV)
            ]
        )

    mine, theirs = piece(head), piece(1 - head)
    near = [[mine, to_partner(theirs)]]
    other = across(theirs)
    straight = [along_inner(mine, k) for k in (1, 2, 3)]
    for k in (1, 2, 3):
        near.append([straight[k - 1], along_y(jnp.where(y + k >= Y, other, near[0][1]), k)])
    near = [half for block in near for half in block]
    own, far, order = cut(queries, output_gradient, span_order, near[3])
    first_far = [cols(x, (1 - head) * KV * COLS, COLS) for x in (queries, output_gradient)]
    far = [[to_partner(x) for x in first_far], [to_partner(far)]]
    far_in = [(along_outer(x, 1),) for x in pack(near, far[0][0], first_far[1])]
    far_out0, near_out0, dq_own0, dq_far0 = attention(0, False, order, own[0], far[0], near, far_in[0])
    back0 = to_partner(dq_far0)
    arrived0 = along_outer(far_out0, -1)
    far_out1, *kept = attention(1, True, order, own[1], far[1], near, far_in[1])
    arrived1 = along_outer(tie(far_out1, arrived0), -1)
    total0, moved0 = send_terms(tie(near_out0, back0), arrived0)
    near_out1, dq_own1, dq_far1 = rest(kept)
    total1, moved1 = send_terms(tie(near_out1, *moved0), arrived1)
    back1 = to_partner(tie(dq_far1, moved1[2]))
    sums = [total0, total1]
    for n, moved in enumerate((moved0, moved1)):
        for x in moved:
            sums[n] = sums[n] + f32(x)
    theirs = to_partner(jnp.stack([bf16(s[SPAN:]) for s in sums]))
    dk, dv = join_terms([bf16(s[:SPAN]) for s in sums], theirs)
    return join_rows((dq_own0, dq_own1), (back0, back1)), dk, dv


def solution(mesh):
    rows = P(("inner", "outer", "head"), None)
    return jax.shard_map(
        shards,
        mesh=mesh,
        in_specs=(rows, rows, rows, rows, P()),
        out_specs=(rows, rows, rows),
        check_vma=False,
    )
```
